32 devices in a mesh: seq: 8 (over z, y), fsdp: 4 (over x, core).
Axes of the slice: x: 2, y: 2, z: 4, core: 2. Of those that a mesh axis runs over, the one named last changes fastest.
Arguments:
- activations: bfloat16 [4, 2048, 640], P('fsdp', 'seq')
- segments: int32 [4, 2048], P('fsdp', 'seq'), may hold values from 0 to 1, as said below
- positions: int32 [4, 2048], P('fsdp', 'seq'), may hold values from 0 to 1535, as said below
- cotangent: bfloat16 [4, 2048, 640], P('fsdp', 'seq'), may hold values from -6 to 6
- query_weight: bfloat16 [2, 640, 1024], P(None, 'fsdp'), may hold values from -0.25 to 0.25
- key_weight: bfloat16 [2, 640, 256], P(None, 'fsdp'), may hold values from -0.25 to 0.25
- value_weight: bfloat16 [2, 640, 256], P(None, 'fsdp'), may hold values from -0.25 to 0.25
- out_weight: bfloat16 [2, 1024, 640], P(None, 'fsdp'), may hold values from -0.375 to 0.375
- gate_weight: bfloat16 [2, 640, 2048], P(None, 'fsdp'), may hold values from -0.25 to 0.25
- up_weight: bfloat16 [2, 640, 2048], P(None, 'fsdp'), may hold values from -0.25 to 0.25
- down_weight: bfloat16 [2, 2048, 640], P(None, 'fsdp'), may hold values from -0.125 to 0.125
- norm_gains: bfloat16 [2, 4, 640], P(None, None, 'fsdp'), may hold values from 0.5 to 1.5
- head_gains: bfloat16 [2, 2, 256], P(None, None, 'fsdp'), may hold values from 0.5 to 1.5
Outputs:
- output: bfloat16 [4, 2048, 640], P('fsdp', 'seq')
- input_grad: bfloat16 [4, 2048, 640], P('fsdp', 'seq')
- query_grad: float32 [2, 640, 1024], P(None, 'fsdp')
- key_grad: float32 [2, 640, 256], P(None, 'fsdp')
- value_grad: float32 [2, 640, 256], P(None, 'fsdp')
- out_grad: float32 [2, 1024, 640], P(None, 'fsdp')
- gate_grad: float32 [2, 640, 2048], P(None, 'fsdp')
- up_grad: float32 [2, 640, 2048], P(None, 'fsdp')
- down_grad: float32 [2, 2048, 640], P(None, 'fsdp')
- norm_gain_grad: float32 [2, 4, 640], P(None, None, 'fsdp')
- head_gain_grad: float32 [2, 2, 256], P(None, None, 'fsdp')
The draws below stay inside these ranges and needn't reach their ends.
Inputs may be any that keep to these rules, and one draw needn't show every extreme that they name: In each group, segments start at 0, never fall and rise by one at each sequence start; each sequence is contiguous. In the first group a sequence starts at token 1024. positions count tokens from 0 at the first token of each sequence.
All inputs are finite; a program needn't handle non-finite values.
Results may differ from the reference program's by a relative error of at most 0.024.
Values may be sent and summed in bfloat16 or wider, within the bound.
A program may use at most 256 MiB of HBM per device.

```python
import jax
import jax.numpy as jnp
from jax import lax

D = 640
HEADS = 4
HD = 256
FF = 2048
WINDOW = 512
LAYERS = 2
GROUPS = 4
GROUP_TOK = 2048
NSEG = 2
QBLOCK = 256


def draw_activations(key, part):
    keys_list = jax.random.split(key, 3)
    row_scale = jnp.exp(jax.random.uniform(keys_list[0], (GROUPS, GROUP_TOK, 1), jnp.float32, -1.15, 1.15))
    col_scale = jnp.exp(jax.random.uniform(keys_list[1], (1, 1, D), jnp.float32, -1.15, 1.15))
    base_vals = jax.random.normal(keys_list[2], (GROUPS, GROUP_TOK, D), jnp.float32)
    return (base_vals * row_scale * col_scale).astype(jnp.bfloat16)


def lengths_for(key, count, total):
    stride = total // count
    jitter = stride // 4
    small = jitter // count
    first_key, second_key = jax.random.split(key, 2)
    longest = jax.random.randint(first_key, (), 0, count).astype(jnp.int32)
    partner = (longest + 1) % count
    drawn = jax.random.randint(second_key, (count,), -small, small + 1).astype(jnp.int32)
    places = jnp.arange(count, dtype=jnp.int32)
    others = jnp.where((places != longest) & (places != partner), drawn, 0)
    remainder = -2 * jitter - jnp.sum(others)
    extra = jnp.where(places == longest, 2 * jitter, jnp.where(places == partner, remainder, others))
    return (stride + extra).astype(jnp.int32)


def segment_layout(key):
    folded = jax.random.fold_in(key, 7)
    half_count = NSEG // 2
    rows_list = []
    for group_at in range(GROUPS):
        group_key = jax.random.fold_in(folded, group_at)
        if group_at == 0:
            if half_count >= 2:
                lower = lengths_for(jax.random.fold_in(group_key, 1), half_count, GROUP_TOK // 2)
                upper = lengths_for(jax.random.fold_in(group_key, 2), half_count, GROUP_TOK // 2)
                rows_list.append(jnp.concatenate([lower, upper], 0))
            else:
                rows_list.append(jnp.full((NSEG,), GROUP_TOK // NSEG, jnp.int32))
        else:
            rows_list.append(lengths_for(group_key, NSEG, GROUP_TOK))
    lengths = jnp.stack(rows_list, 0)
    starts = jnp.cumsum(lengths, 1)[:, :-1].astype(jnp.int32)
    places = jnp.arange(GROUP_TOK, dtype=jnp.int32)[None, :, None]
    passed = places >= starts[:, None, :]
    seg_ids = jnp.sum(passed.astype(jnp.int32), -1)
    begins = jnp.max(jnp.where(passed, starts[:, None, :], 0), -1)
    return (seg_ids.astype(jnp.int32), (places[..., 0] - begins).astype(jnp.int32))


def draw_segments(key, part):
    return segment_layout(key)[0]


def draw_positions(key, part):
    return segment_layout(key)[1]


def level_of(own_key, extent, cuts, smallest, high):
    loudness, own = 1.0, jax.random.fold_in(own_key, 6)
    for position, blocks in cuts:
        steps = jnp.exp(jax.random.uniform(jax.random.fold_in(own, position), (blocks,), jnp.float32, smallest / len(cuts), high / len(cuts)))
        loudness = loudness * jnp.repeat(steps, extent[position] // blocks).reshape([-1 if axis == position else 1 for axis in range(len(extent))])
    return loudness


def centred(rng, shape, deviation, limit, shards=(), kind=jnp.bfloat16):
    result = jax.random.normal(rng, shape, jnp.float32) * deviation
    if len(shards) > 0:
        result = level_of(rng, shape, shards, -0.22, 0.18) * result
    return jnp.clip(result, min=-limit, max=limit).astype(kind)


def setup_inputs(seed: int = 0) -> dict:
    arg_keys = jax.random.split(jax.random.key(seed), 14)
    activations = draw_activations(jax.random.fold_in(arg_keys[13], 71), 0)
    segments = draw_segments(jax.random.fold_in(arg_keys[13], 71), 0)
    positions = draw_positions(jax.random.fold_in(arg_keys[13], 71), 0)
    cotangent = centred(arg_keys[3], (GROUPS, GROUP_TOK, D), 1.0, 6.0, ((0, 4), (1, 8)))
    query_weight = centred(arg_keys[4], (LAYERS, D, HEADS * HD), D ** -0.5, 0.25, ((1, 4),))
    key_weight = centred(arg_keys[5], (LAYERS, D, HD), D ** -0.5, 0.25, ((1, 4),))
    value_weight = centred(arg_keys[6], (LAYERS, D, HD), D ** -0.5, 0.25, ((1, 4),))
    out_weight = centred(arg_keys[7], (LAYERS, HEADS * HD, D), HD ** -0.5, 0.375, ((1, 4),))
    gate_weight = centred(arg_keys[8], (LAYERS, D, FF), D ** -0.5, 0.25, ((1, 4),))
    up_weight = centred(arg_keys[9], (LAYERS, D, FF), D ** -0.5, 0.25, ((1, 4),))
    down_weight = centred(arg_keys[10], (LAYERS, FF, D), FF ** -0.5, 0.125, ((1, 4),))
    norm_gains = jnp.clip(1.0 + 0.1 * jax.random.normal(arg_keys[11], (LAYERS, 4, D), jnp.float32), 0.5, 1.5).astype(jnp.bfloat16)
    head_gains = jnp.clip(1.0 + 0.1 * jax.random.normal(arg_keys[12], (LAYERS, 2, HD), jnp.float32), 0.5, 1.5).astype(jnp.bfloat16)
    return dict(activations=activations, segments=segments, positions=positions, cotangent=cotangent, query_weight=query_weight, key_weight=key_weight, value_weight=value_weight, out_weight=out_weight, gate_weight=gate_weight, up_weight=up_weight, down_weight=down_weight, norm_gains=norm_gains, head_gains=head_gains)


EPS = 1e-06
HIGH = lax.Precision.HIGHEST

@jax.custom_vjp
def low(v):
    return lax.optimization_barrier(v.astype(jnp.bfloat16)).astype(jnp.float32)

@jax.custom_vjp
def low_back(v):
    return v

def low_keep(v):
    return (low(v), None)

def low_pass(kept, grad):
    return (grad,)

def back_keep(v):
    return (v, None)

def back_low(kept, grad):
    return (low(grad),)
low.defvjp(low_keep, low_pass)
low_back.defvjp(back_keep, back_low)

def rms_scale(values, gain_vec):
    return values * lax.rsqrt(lax.optimization_barrier(jnp.mean(values * values, -1, keepdims=True)) + EPS) * gain_vec

def rotate(values, cosine, sine_part):
    middle_at = values.shape[-1] // 2
    leading = values[..., :middle_at]
    trailing = values[..., middle_at:]
    return jnp.concatenate([leading * cosine - trailing * sine_part, trailing * cosine + leading * sine_part], -1)

def angles(places):
    halfway = HD // 2
    frequency = 10000.0 ** (-(jnp.arange(halfway, dtype=jnp.float32) * 2.0 / HD))
    turned = places.astype(jnp.float32)[:, None] * frequency[None, :]
    return (jnp.cos(turned), jnp.sin(turned))

def matmul(first_op, second_op):
    return jnp.dot(first_op, second_op, precision=HIGH, preferred_element_type=jnp.float32)

def block_attend(query_block, key_slab, value_slab, seg_query, seg_key):
    scores = low_back(jnp.einsum('qhd,kd->hqk', query_block, key_slab, precision=HIGH) * HD ** (-0.5))
    row_count = query_block.shape[0]
    span_keys = key_slab.shape[0]
    distance = jnp.arange(row_count, dtype=jnp.int32)[:, None] - jnp.arange(span_keys, dtype=jnp.int32)[None, :] + WINDOW
    allowed = ((distance >= 0) & (distance < WINDOW) & (seg_query[:, None] == seg_key[None, :]))[None]
    masked = jnp.where(allowed, scores, -1e+30)
    row_top = lax.optimization_barrier(jnp.max(masked, -1, keepdims=True))
    raised = jnp.where(allowed, jnp.exp(masked - row_top), 0.0)
    attention = low(raised / lax.optimization_barrier(jnp.sum(raised, -1, keepdims=True)))
    return jnp.einsum('hqk,kd->qhd', attention, value_slab, precision=HIGH)

def attend(query_rot, key_rot, values, seg_all):
    count_rows = query_rot.shape[0]
    blocks_n = count_rows // QBLOCK
    key_pad = jnp.concatenate([jnp.zeros((WINDOW, HD), key_rot.dtype), key_rot], 0)
    value_pad = jnp.concatenate([jnp.zeros((WINDOW, HD), values.dtype), values], 0)
    seg_pad = jnp.concatenate([jnp.full((WINDOW,), -1, jnp.int32), seg_all], 0)

    @jax.checkpoint
    def one_block(block_index):
        begin_at = (block_index * QBLOCK).astype(jnp.int32)
        query_block = lax.dynamic_slice_in_dim(query_rot, begin_at, QBLOCK, 0)
        key_slab = lax.dynamic_slice_in_dim(key_pad, begin_at, QBLOCK + WINDOW, 0)
        value_slab = lax.dynamic_slice_in_dim(value_pad, begin_at, QBLOCK + WINDOW, 0)
        seg_query = lax.dynamic_slice_in_dim(seg_all, begin_at, QBLOCK, 0)
        seg_key = lax.dynamic_slice_in_dim(seg_pad, begin_at, QBLOCK + WINDOW, 0)
        return block_attend(query_block, key_slab, value_slab, seg_query, seg_key)
    blocks_out = lax.map(one_block, jnp.arange(blocks_n, dtype=jnp.int32))
    return blocks_out.reshape(count_rows, HEADS, HD)

def layer_forward(x, query_w, key_w, value_w, out_w, gate_w, up_w, down_w, model_gains, head_pair, seg_all, cosine, sine_part):
    count_rows = x.shape[0]
    hidden = low(rms_scale(x, model_gains[0]))
    query_raw = low_back(matmul(hidden, query_w)).reshape(count_rows, HEADS, HD)
    key_raw = low_back(matmul(hidden, key_w))
    values = low(low_back(matmul(hidden, value_w)))
    query_rot = low(rotate(rms_scale(query_raw, head_pair[0]), cosine[:, None, :], sine_part[:, None, :]))
    key_rot = low(rotate(rms_scale(key_raw, head_pair[1]), cosine, sine_part))
    attended = low(low_back(attend(query_rot, key_rot, values, seg_all))).reshape(count_rows, HEADS * HD)
    projected = low_back(matmul(attended, out_w))
    middle = x + rms_scale(projected, model_gains[1])
    hidden_two = low(rms_scale(middle, model_gains[2]))
    gate_vals = low_back(matmul(hidden_two, gate_w))
    up_part = low_back(matmul(hidden_two, up_w))
    activated = low(jax.nn.gelu(gate_vals, approximate=True) * up_part)
    ffn_out = low_back(matmul(activated, down_w))
    return middle + rms_scale(ffn_out, model_gains[3])

def reference(activations, segments, positions, cotangent, query_weight, key_weight, value_weight, out_weight, gate_weight, up_weight, down_weight, norm_gains, head_gains):
    total_rows = GROUPS * GROUP_TOK
    seg_all = (segments + jnp.arange(GROUPS, dtype=jnp.int32)[:, None] * NSEG).reshape(total_rows).astype(jnp.int32)
    cosine, sine_part = angles(positions.reshape(total_rows))
    start_x = activations.reshape(total_rows, D).astype(jnp.float32)
    params = (query_weight.astype(jnp.float32), key_weight.astype(jnp.float32), value_weight.astype(jnp.float32), out_weight.astype(jnp.float32), gate_weight.astype(jnp.float32), up_weight.astype(jnp.float32), down_weight.astype(jnp.float32), norm_gains.astype(jnp.float32), head_gains.astype(jnp.float32))

    def run(stream, query_w, key_w, value_w, out_w, gate_w, up_w, down_w, model_g, head_g):
        for layer_at in range(LAYERS):
            stream = layer_forward(stream, query_w[layer_at], key_w[layer_at], value_w[layer_at], out_w[layer_at], gate_w[layer_at], up_w[layer_at], down_w[layer_at], model_g[layer_at], head_g[layer_at], seg_all, cosine, sine_part)
        return stream
    outcome, pullback = jax.vjp(run, start_x, *params)
    grads = pullback(cotangent.reshape(total_rows, D).astype(jnp.float32))
    return (outcome.astype(jnp.bfloat16).reshape(GROUPS, GROUP_TOK, D), grads[0].astype(jnp.bfloat16).reshape(GROUPS, GROUP_TOK, D), grads[1], grads[2], grads[3], grads[4], grads[5], grads[6], grads[7], grads[8], grads[9])
```

```python
import jax
import jax.numpy as jnp
from jax import lax
from jax.sharding import PartitionSpec as P

HEADS = 4
HD = 256
WINDOW = 512


EPS = 1e-06


def passed_along(value, axis, steps):
    count = lax.axis_size(axis)
    first, last = (max(0, -steps), min(count, count - steps))
    return lax.ppermute(value, axis, [(source, source + steps) for source in range(first, last)])


def swapped(value, axis, bit):
    count = lax.axis_size(axis)
    return lax.ppermute(value, axis, [(source, source ^ bit) for source in range(count)])


def axis_bits(axis):
    bits = []
    bit = 1
    while bit < lax.axis_size(axis):
        bits.append(bit)
        bit = 2 * bit
    return bits


def chosen(value, at, dim):
    return lax.dynamic_index_in_dim(value, at, dim, keepdims=False)


def added(first_op, second_op):
    return (first_op.astype(jnp.float32) + second_op.astype(jnp.float32)).astype(jnp.bfloat16)


def summed_shard(term):
    shards = lax.axis_size("fsdp")
    index = lax.axis_index("fsdp")
    part = term.reshape(shards, term.shape[0] // shards, term.shape[1])
    for bit in axis_bits("fsdp"):
        mine = (index // bit) % 2
        pairs = part.reshape(part.shape[0] // 2, 2, part.shape[1], part.shape[2])
        got = swapped(chosen(pairs, 1 - mine, 1), "fsdp", bit)
        part = added(chosen(pairs, mine, 1), got)
    part = part[0]
    blocks = lax.axis_size("seq")
    index = lax.axis_index("seq")
    dim = 0 if part.shape[0] % (16 * blocks) == 0 else 1
    for bit in axis_bits("seq"):
        mine = (index // bit) % 2
        half = part.shape[dim] // 2
        away = lax.dynamic_slice_in_dim(part, (1 - mine) * half, half, dim)
        got = swapped(away, "seq", bit)
        part = added(lax.dynamic_slice_in_dim(part, mine * half, half, dim), got)
    for bit in axis_bits("seq")[::-1]:
        first = (index // bit) % 2 == 0
        got = swapped(part, "seq", bit)
        part = jnp.concatenate([jnp.where(first, part, got), jnp.where(first, got, part)], dim)
    return part.astype(jnp.float32)


def summed_everywhere(values):
    for axis in ("fsdp", "seq"):
        for bit in axis_bits(axis):
            values = values + swapped(values, axis, bit)
    return values


def rms_scale(values, gain_vec):
    return values * lax.rsqrt(jnp.mean(values * values, -1, keepdims=True) + EPS) * gain_vec


def rotate(values, cosine, sine_part):
    middle_at = values.shape[-1] // 2
    leading = values[..., :middle_at]
    trailing = values[..., middle_at:]
    return jnp.concatenate(
        [leading * cosine - trailing * sine_part, trailing * cosine + leading * sine_part], -1
    )


def angles(places):
    halfway = HD // 2
    frequency = 10000.0 ** (-(jnp.arange(halfway, dtype=jnp.float32) * 2.0 / HD))
    turned = places.astype(jnp.float32)[:, None] * frequency[None, :]
    return (jnp.cos(turned), jnp.sin(turned))


def gelu_gate(gate_vals, up_part):
    return jax.nn.gelu(gate_vals, approximate=True) * up_part


def outer_sum(first_op, second_op):
    return lax.dot_general(
        first_op, second_op, (((0,), (0,)), ((), ())), preferred_element_type=jnp.float32
    )


def back_dot(first_op, second_op):
    return lax.dot_general(
        first_op, second_op, (((1,), (1,)), ((), ())), preferred_element_type=jnp.float32
    )


def rim_sizes(tokens):
    reach = (WINDOW + tokens - 1) // tokens
    return [
        (shift_by, min(tokens, WINDOW - (shift_by - 1) * tokens))
        for shift_by in range(reach, 0, -1)
    ]


def block_scores(query_block, key_slab, seg_query, seg_key):
    scores = jnp.einsum(
        "qhd,kd->hqk", query_block, key_slab, preferred_element_type=jnp.float32
    ) * HD ** (-0.5)
    row_count = query_block.shape[0]
    span_keys = key_slab.shape[0]
    distance = (
        jnp.arange(row_count, dtype=jnp.int32)[:, None]
        - jnp.arange(span_keys, dtype=jnp.int32)[None, :]
        + WINDOW
    )
    allowed = (distance >= 0) & (distance < WINDOW) & (seg_query[:, None] == seg_key[None, :])
    return (scores, allowed[None])


def forward_layer(x, weights_now, seg_own, seg_ext, cosine, sine_part):
    qkv_mat, out_mat, both_mat, down_mat, model_gains, head_pair = weights_now
    tokens = x.shape[0]
    gains_now = model_gains.astype(jnp.float32)
    head_now = head_pair.astype(jnp.float32)
    normed, pull_in = jax.vjp(rms_scale, x, gains_now[0])
    hidden = normed.astype(jnp.bfloat16)
    raw_all = jnp.dot(hidden, qkv_mat, preferred_element_type=jnp.float32)
    query_raw = raw_all[:, : HEADS * HD]
    key_raw = raw_all[:, HEADS * HD : HEADS * HD + HD]
    values = raw_all[:, HEADS * HD + HD :].astype(jnp.bfloat16)

    def query_piece(raw_vals, gain_vec):
        return rotate(
            rms_scale(raw_vals.reshape(tokens, HEADS, HD), gain_vec),
            cosine[:, None, :],
            sine_part[:, None, :],
        )

    def key_piece(raw_vals, gain_vec):
        return rotate(rms_scale(raw_vals, gain_vec), cosine, sine_part)

    query_rot, pull_query = jax.vjp(query_piece, query_raw, head_now[0])
    key_rot, pull_key = jax.vjp(key_piece, key_raw, head_now[1])
    query_low = query_rot.astype(jnp.bfloat16)
    key_low = key_rot.astype(jnp.bfloat16)
    key_parts = []
    value_parts = []
    for shift_by, rim_rows in rim_sizes(tokens):
        got_key, got_value = passed_along((key_low, values), "seq", shift_by)
        key_parts.append(got_key)
        value_parts.append(got_value)
    key_ext = jnp.concatenate(key_parts + [key_low], 0)
    value_ext = jnp.concatenate(value_parts + [values], 0)
    scores, allowed = block_scores(query_low, key_ext, seg_own, seg_ext)
    masked = jnp.where(allowed, scores, -1e30)
    row_top = jnp.max(masked, -1, keepdims=True)
    raised = jnp.where(allowed, jnp.exp(masked - row_top), 0.0)
    row_total = jnp.sum(raised, -1, keepdims=True)
    attention = (raised / row_total).astype(jnp.bfloat16)
    outputs = jnp.einsum("hqk,kd->qhd", attention, value_ext, preferred_element_type=jnp.float32)
    row_tops = [row_top]
    totals = [row_total]
    attended = outputs.reshape(tokens, HEADS * HD).astype(jnp.bfloat16)
    projected = jnp.dot(attended, out_mat, preferred_element_type=jnp.float32)
    post_out, pull_post = jax.vjp(rms_scale, projected, gains_now[1])
    middle = x + post_out
    normed_two, pull_pre = jax.vjp(rms_scale, middle, gains_now[2])
    hidden_two = normed_two.astype(jnp.bfloat16)
    both_vals = jnp.dot(hidden_two, both_mat, preferred_element_type=jnp.float32)
    gate_vals = both_vals[:, : both_vals.shape[1] // 2]
    up_part = both_vals[:, both_vals.shape[1] // 2 :]
    activated, pull_act = jax.vjp(gelu_gate, gate_vals, up_part)
    act_low = activated.astype(jnp.bfloat16)
    ffn_out = jnp.dot(act_low, down_mat, preferred_element_type=jnp.float32)
    post_two, pull_ffn = jax.vjp(rms_scale, ffn_out, gains_now[3])
    retained = (
        hidden,
        query_low,
        key_ext,
        value_ext,
        row_tops,
        totals,
        attended,
        hidden_two,
        act_low,
        pull_in,
        pull_query,
        pull_key,
        pull_post,
        pull_pre,
        pull_act,
        pull_ffn,
    )
    return (middle + post_two, retained)


def backward_layer(upstream, weights_now, retained, seg_own, seg_ext):
    qkv_mat, out_mat, both_mat, down_mat, model_gains, head_pair = weights_now
    (
        hidden,
        query_low,
        key_ext,
        value_ext,
        row_tops,
        totals,
        attended,
        hidden_two,
        act_low,
        pull_in,
        pull_query,
        pull_key,
        pull_post,
        pull_pre,
        pull_act,
        pull_ffn,
    ) = retained
    tokens = upstream.shape[0]
    block_rows = min(512, tokens)
    grad_ffn, gain_ffn = pull_ffn(upstream)
    ffn_low = grad_ffn.astype(jnp.bfloat16)
    down_grad = summed_shard(outer_sum(act_low, ffn_low).astype(jnp.bfloat16))
    grad_act = back_dot(ffn_low, down_mat)
    grad_gate, grad_up = pull_act(grad_act)
    both_low = jnp.concatenate([grad_gate, grad_up], 1).astype(jnp.bfloat16)
    both_grad = summed_shard(outer_sum(hidden_two, both_low).astype(jnp.bfloat16))
    grad_hidden_two = back_dot(both_low, both_mat)
    middle_part, gain_pre = pull_pre(grad_hidden_two)
    grad_middle = upstream + middle_part
    grad_proj, gain_post = pull_post(grad_middle)
    proj_low = grad_proj.astype(jnp.bfloat16)
    out_grad = summed_shard(outer_sum(attended, proj_low).astype(jnp.bfloat16))
    grad_att = back_dot(proj_low, out_mat).astype(jnp.bfloat16).reshape(tokens, HEADS, HD)
    key_back = jnp.zeros(key_ext.shape, jnp.float32)
    value_back = jnp.zeros(value_ext.shape, jnp.float32)
    query_parts = []
    for number, begin_at in enumerate(range(0, tokens, block_rows)):
        span_keys = block_rows + WINDOW
        scores, allowed = block_scores(query_low, key_ext, seg_own, seg_ext)
        masked = jnp.where(allowed, scores, -1e30)
        raised = jnp.where(allowed, jnp.exp(masked - row_tops[number]), 0.0)
        attention = raised / totals[number]
        attention_low = attention.astype(jnp.bfloat16)
        grad_prob = jnp.einsum(
            "qhd,kd->hqk", grad_att, value_ext, preferred_element_type=jnp.float32
        )
        spread = jnp.sum(grad_prob * attention, -1, keepdims=True)
        grad_scores = (attention * (grad_prob - spread)).astype(jnp.bfloat16)
        query_parts.append(
            jnp.einsum("hqk,kd->qhd", grad_scores, key_ext, preferred_element_type=jnp.float32)
            * HD ** (-0.5)
        )
        key_back = key_back.at[begin_at : begin_at + span_keys].add(
            jnp.einsum("hqk,qhd->kd", grad_scores, query_low, preferred_element_type=jnp.float32)
            * HD ** (-0.5)
        )
        value_back = value_back.at[begin_at : begin_at + span_keys].add(
            jnp.einsum("hqk,qhd->kd", attention_low, grad_att, preferred_element_type=jnp.float32)
        )
    key_own = key_back[WINDOW:]
    value_own = value_back[WINDOW:]
    offset = 0
    for shift_by, rim_rows in rim_sizes(tokens):
        got_key, got_value = (
            passed_along(
                key_back[offset : offset + rim_rows].astype(jnp.bfloat16), "seq", -shift_by
            ).astype(jnp.float32),
            passed_along(
                value_back[offset : offset + rim_rows].astype(jnp.bfloat16), "seq", -shift_by
            ).astype(jnp.float32),
        )
        key_own = key_own.at[tokens - rim_rows :].add(got_key)
        value_own = value_own.at[tokens - rim_rows :].add(got_value)
        offset = offset + rim_rows
    grad_query, gain_query = pull_query(query_parts[0])
    grad_key, gain_key = pull_key(key_own)
    qkv_low = jnp.concatenate(
        [
            grad_query.astype(jnp.bfloat16),
            grad_key.astype(jnp.bfloat16),
            value_own.astype(jnp.bfloat16),
        ],
        1,
    )
    qkv_grad = summed_shard(outer_sum(hidden, qkv_low).astype(jnp.bfloat16))
    grad_hidden = back_dot(qkv_low, qkv_mat)
    grad_input, gain_in = pull_in(grad_hidden)
    gain_terms = jnp.concatenate([gain_in, gain_post, gain_pre, gain_ffn, gain_query, gain_key])
    query_cols = HEADS * HD
    ffn_cols = both_grad.shape[1] // 2
    shards = (
        qkv_grad[:, :query_cols],
        qkv_grad[:, query_cols : query_cols + HD],
        qkv_grad[:, query_cols + HD :],
        out_grad,
        both_grad[:, :ffn_cols],
        both_grad[:, ffn_cols:],
        down_grad,
    )
    return (grad_middle + grad_input, shards, summed_everywhere(gain_terms))


def local(
    activations,
    segments,
    positions,
    cotangent,
    query_weight,
    key_weight,
    value_weight,
    out_weight,
    gate_weight,
    up_weight,
    down_weight,
    norm_gains,
    head_gains,
):
    tokens = activations.shape[1]
    layers = query_weight.shape[0]
    fsdp_size = lax.axis_size("fsdp")
    seg_own = segments[0]
    seg_parts = []
    for shift_by, rim_rows in rim_sizes(tokens):
        seg_parts.append(passed_along(seg_own + 1, "seq", shift_by) - 1)
    seg_ext = jnp.concatenate(seg_parts + [seg_own], 0)
    cosine, sine_part = angles(positions[0])
    stream = activations[0].astype(jnp.float32)
    width = norm_gains.shape[2]
    head_width = head_gains.shape[2]
    gain_cols = jnp.concatenate(
        [
            norm_gains.reshape(layers * 4, width).T,
            jnp.pad(head_gains.reshape(layers * 2, head_width).T, ((0, width - head_width), (0, 0))),
        ],
        1,
    )

    def gathered(part):
        return lax.all_gather(part, "fsdp", axis=0, tiled=True)

    stored = []
    for layer_at in range(layers):
        qkv_parts = [query_weight[layer_at], key_weight[layer_at], value_weight[layer_at]]
        if layer_at == 0:
            qkv_parts.append(gain_cols)
        qkv_mat = gathered(jnp.concatenate(qkv_parts, 1))
        if layer_at == 0:
            gains_all = qkv_mat[:, (HEADS + 2) * HD :].astype(jnp.float32)
            model_all = gains_all[:, : layers * 4].T.reshape(layers, 4, -1)
            head_all = gains_all.reshape(fsdp_size, width, -1)[:, :head_width, layers * 4 :]
            head_all = head_all.reshape(HD, layers * 2).T.reshape(layers, 2, HD)
            qkv_mat = qkv_mat[:, : (HEADS + 2) * HD]
        weights_now = (
            qkv_mat,
            gathered(out_weight[layer_at]),
            gathered(jnp.concatenate([gate_weight[layer_at], up_weight[layer_at]], 1)),
            gathered(down_weight[layer_at]),
            model_all[layer_at],
            head_all[layer_at],
        )
        stream, retained = forward_layer(stream, weights_now, seg_own, seg_ext, cosine, sine_part)
        stored.append((weights_now, retained))
    output = stream.astype(jnp.bfloat16)
    upstream = cotangent[0].astype(jnp.float32)
    collected = [None] * layers
    fsdp_at = lax.axis_index("fsdp")
    for layer_at in range(layers - 1, -1, -1):
        weights_now, retained = stored[layer_at]
        upstream, shards, gain_sums = backward_layer(
            upstream, weights_now, retained, seg_own, seg_ext
        )
        model_width = 4 * fsdp_size * width
        model_shard = lax.dynamic_slice_in_dim(
            gain_sums[:model_width].reshape(4, -1), fsdp_at * width, width, 1
        )
        head_shard = lax.dynamic_slice_in_dim(
            gain_sums[model_width:].reshape(2, -1), fsdp_at * head_width, head_width, 1
        )
        collected[layer_at] = (shards, model_shard, head_shard)
    input_grad = upstream.astype(jnp.bfloat16)
    stacked = [
        jnp.stack([collected[layer_at][0][number] for layer_at in range(layers)])
        for number in range(7)
    ]
    model_grad = jnp.stack([collected[layer_at][1] for layer_at in range(layers)])
    head_grad = jnp.stack([collected[layer_at][2] for layer_at in range(layers)])
    return (
        output[None],
        input_grad[None],
        stacked[0],
        stacked[1],
        stacked[2],
        stacked[3],
        stacked[4],
        stacked[5],
        stacked[6],
        model_grad,
        head_grad,
    )


def solution(mesh):
    placed = (
        P("fsdp", "seq", None),
        P("fsdp", "seq"),
        P("fsdp", "seq"),
        P("fsdp", "seq", None),
        P(None, "fsdp", None),
        P(None, "fsdp", None),
        P(None, "fsdp", None),
        P(None, "fsdp", None),
        P(None, "fsdp", None),
        P(None, "fsdp", None),
        P(None, "fsdp", None),
        P(None, None, "fsdp"),
        P(None, None, "fsdp"),
    )
    return jax.shard_map(
        local,
        mesh=mesh,
        in_specs=placed,
        out_specs=(
            P("fsdp", "seq", None),
            P("fsdp", "seq", None),
            P(None, "fsdp", None),
            P(None, "fsdp", None),
            P(None, "fsdp", None),
            P(None, "fsdp", None),
            P(None, "fsdp", None),
            P(None, "fsdp", None),
            P(None, "fsdp", None),
            P(None, None, "fsdp"),
            P(None, None, "fsdp"),
        ),
        check_vma=False,
    )
```

```python
import functools

import jax
import jax.numpy as jnp
from jax import lax
from jax.experimental import pallas as pl
from jax.experimental.pallas import tpu as pltpu
from jax.sharding import PartitionSpec as P

HEADS = 4
HD = 256
WINDOW = 512
VMEM_MIB = 58


EPS = 1e-06


def passed_along(value, axis, steps):
    count = lax.axis_size(axis)
    first, last = (max(0, -steps), min(count, count - steps))
    return lax.ppermute(value, axis, [(source, source + steps) for source in range(first, last)])


def swapped(value, axis, bit):
    count = lax.axis_size(axis)
    return lax.ppermute(value, axis, [(source, source ^ bit) for source in range(count)])


def axis_bits(axis):
    bits = []
    bit = 1
    while bit < lax.axis_size(axis):
        bits.append(bit)
        bit = 2 * bit
    return bits


def chosen(value, at, dim):
    return lax.dynamic_index_in_dim(value, at, dim, keepdims=False)


def added(first_op, second_op):
    return (first_op.astype(jnp.float32) + second_op.astype(jnp.float32)).astype(jnp.bfloat16)


def summed_shard(term):
    shards = lax.axis_size("fsdp")
    index = lax.axis_index("fsdp")
    part = term.reshape(shards, term.shape[0] // shards, term.shape[1])
    for bit in axis_bits("fsdp"):
        mine = (index // bit) % 2
        pairs = part.reshape(part.shape[0] // 2, 2, part.shape[1], part.shape[2])
        got = swapped(chosen(pairs, 1 - mine, 1), "fsdp", bit)
        part = added(chosen(pairs, mine, 1), got)
    part = part[0]
    blocks = lax.axis_size("seq")
    index = lax.axis_index("seq")
    dim = 0 if part.shape[0] % (16 * blocks) == 0 else 1
    for bit in axis_bits("seq"):
        mine = (index // bit) % 2
        half = part.shape[dim] // 2
        away = lax.dynamic_slice_in_dim(part, (1 - mine) * half, half, dim)
        got = swapped(away, "seq", bit)
        part = added(lax.dynamic_slice_in_dim(part, mine * half, half, dim), got)
    for bit in axis_bits("seq")[::-1]:
        first = (index // bit) % 2 == 0
        got = swapped(part, "seq", bit)
        part = jnp.concatenate([jnp.where(first, part, got), jnp.where(first, got, part)], dim)
    return part.astype(jnp.float32)


def part_of(ref, dim, begin_at, size):
    if dim == 0:
        return ref.at[pl.ds(pl.multiple_of(begin_at, 16), size), :]
    return ref.at[:, pl.ds(pl.multiple_of(begin_at, 128), size)]


def add_into(target, first_op, second_op):
    step = 32

    def body(number, carry):
        rows = pl.ds(pl.multiple_of(number * step, step), step)
        target[rows, :] = (
            first_op[rows, :].astype(jnp.float32) + second_op[rows, :].astype(jnp.float32)
        ).astype(jnp.bfloat16)
        return carry

    lax.fori_loop(0, target.shape[0] // step, body, 0)


def reduce_kernel(dims, bits, *refs):
    count = len(dims)
    levels = len(bits)
    terms, sums = refs[:count], refs[count : 2 * count]
    refs = refs[2 * count :]
    halves, shards = refs[:count], refs[count : 2 * count]
    slots = refs[2 * count : (2 + levels) * count]
    send_sem, recv_sem = refs[-2:]
    at_f = lax.axis_index("fsdp")
    at_s = lax.axis_index("seq")
    core, far = at_f % 2, at_f // 2
    core_peer = {"fsdp": at_f + 1 - 2 * core}
    far_peer = {"fsdp": at_f + 2 - 4 * far}
    mine = [(at_s // bit) % 2 for bit in bits]
    seq_peers = [{"seq": at_s + bit - 2 * bit * one} for bit, one in zip(bits, mine)]
    barrier = pltpu.get_barrier_semaphore()
    for peer in [core_peer, far_peer] + seq_peers:
        pl.semaphore_signal(barrier, inc=1, device_id=peer, device_id_type=pl.DeviceIdType.MESH)
    pl.semaphore_wait(barrier, 2 + levels)

    stages = 2 + 2 * levels
    flying = {}

    def offset(group, level):
        size = shards[group].shape[dims[group]]
        total = 0
        for done in range(level):
            size = size // 2
            total = total + mine[done] * size
        return total, size

    def send(group, stage, source, target, peer):
        copy = pltpu.make_async_remote_copy(
            src_ref=source,
            dst_ref=target,
            send_sem=send_sem.at[group, stage],
            recv_sem=recv_sem.at[group, stage],
            device_id=peer,
            device_id_type=pl.DeviceIdType.MESH,
        )
        copy.start()
        flying[group] = copy

    def begin(group, stage):
        dim = dims[group]
        if stage == 0:
            send(group, stage, terms[group].at[:, 1 - core], halves[group], core_peer)
        elif stage == 1:
            send(group, stage, halves[group].at[1 - far], shards[group], far_peer)
        elif stage < 2 + levels:
            level = stage - 2
            start, size = offset(group, level)
            half = size // 2
            source = part_of(shards[group], dim, start + (1 - mine[level]) * half, half)
            send(group, stage, source, slots[level * count + group], seq_peers[level])
        else:
            level = stages - 1 - stage
            start, size = offset(group, level + 1)
            piece = part_of(sums[group], dim, start, size)
            send(group, stage, piece, piece, seq_peers[level])

    def finish(group, stage):
        dim = dims[group]
        flying[group].wait()
        if stage == 0:
            for number in range(2):
                half = halves[group].at[number]
                add_into(half, terms[group].at[number, core], half)
        elif stage == 1:
            add_into(shards[group], halves[group].at[far], shards[group])
        elif stage < 2 + levels:
            level = stage - 2
            start, size = offset(group, level + 1)
            kept = part_of(shards[group], dim, start, size)
            target = part_of(sums[group], dim, start, size) if level == levels - 1 else kept
            add_into(target, kept, slots[level * count + group])

    for tick in range(count + stages):
        for group in reversed(range(count)):
            stage = tick - group
            if 1 <= stage <= stages:
                finish(group, stage - 1)
            if 0 <= stage < stages:
                begin(group, stage)


def summed_shards(terms):
    fsdp_size, seq_size = lax.axis_size("fsdp"), lax.axis_size("seq")
    dims = []
    for term in terms:
        rows, cols = term.shape[0] // fsdp_size, term.shape[1]
        if rows % (32 * seq_size) == 0:
            dims.append(0)
        elif rows % 32 == 0 and cols % (128 * seq_size) == 0:
            dims.append(1)
    if fsdp_size != 4 or len(dims) < len(terms):
        return [summed_shard(term) for term in terms]
    bits = axis_bits("seq")
    views = [term.reshape(2, 2, term.shape[0] // 4, term.shape[1]) for term in terms]
    shapes = [view.shape[2:] for view in views]
    scratch = [pltpu.VMEM((2,) + shape, jnp.bfloat16) for shape in shapes]
    scratch += [pltpu.VMEM(shape, jnp.bfloat16) for shape in shapes]
    for bit in bits:
        for (rows, cols), dim in zip(shapes, dims):
            piece = (rows // (2 * bit), cols) if dim == 0 else (rows, cols // (2 * bit))
            scratch.append(pltpu.VMEM(piece, jnp.bfloat16))
    flights = (len(terms), 2 + 2 * len(bits))
    scratch += [pltpu.SemaphoreType.DMA(flights), pltpu.SemaphoreType.DMA(flights)]
    sums = pl.pallas_call(
        functools.partial(reduce_kernel, tuple(dims), tuple(bits)),
        out_shape=[jax.ShapeDtypeStruct(shape, jnp.bfloat16) for shape in shapes],
        in_specs=[pl.BlockSpec(memory_space=pltpu.VMEM)] * len(terms),
        out_specs=[pl.BlockSpec(memory_space=pltpu.VMEM)] * len(terms),
        scratch_shapes=scratch,
        compiler_params=pltpu.CompilerParams(
            collective_id=0, has_side_effects=True, vmem_limit_bytes=VMEM_MIB * 2**20
        ),
    )(*views)
    return [value.astype(jnp.float32) for value in sums]


def rms_scale(values, gain_vec):
    return values * lax.rsqrt(jnp.mean(values * values, -1, keepdims=True) + EPS) * gain_vec


def rotate(values, cosine, sine_part):
    middle_at = values.shape[-1] // 2
    leading = values[..., :middle_at]
    trailing = values[..., middle_at:]
    return jnp.concatenate(
        [leading * cosine - trailing * sine_part, trailing * cosine + leading * sine_part], -1
    )


def angles(places):
    halfway = HD // 2
    frequency = 10000.0 ** (-(jnp.arange(halfway, dtype=jnp.float32) * 2.0 / HD))
    turned = places.astype(jnp.float32)[:, None] * frequency[None, :]
    return (jnp.cos(turned), jnp.sin(turned))


def gelu_gate(gate_vals, up_part):
    return jax.nn.gelu(gate_vals, approximate=True) * up_part


def outer_sum(first_op, second_op):
    return lax.dot_general(
        first_op, second_op, (((0,), (0,)), ((), ())), preferred_element_type=jnp.float32
    )


def back_dot(first_op, second_op):
    return lax.dot_general(
        first_op, second_op, (((1,), (1,)), ((), ())), preferred_element_type=jnp.float32
    )


def rim_sizes(tokens):
    reach = (WINDOW + tokens - 1) // tokens
    return [
        (shift_by, min(tokens, WINDOW - (shift_by - 1) * tokens))
        for shift_by in range(reach, 0, -1)
    ]


def block_scores(query_block, key_slab, seg_query, seg_key):
    scores = jnp.einsum(
        "qhd,kd->hqk", query_block, key_slab, preferred_element_type=jnp.float32
    ) * HD ** (-0.5)
    row_count = query_block.shape[0]
    span_keys = key_slab.shape[0]
    distance = (
        jnp.arange(row_count, dtype=jnp.int32)[:, None]
        - jnp.arange(span_keys, dtype=jnp.int32)[None, :]
        + WINDOW
    )
    allowed = (distance >= 0) & (distance < WINDOW) & (seg_query[:, None] == seg_key[None, :])
    return (scores, allowed[None])


def forward_layer(x, weights_now, seg_own, seg_ext, cosine, sine_part):
    qkv_mat, out_mat, both_mat, down_mat, model_gains, head_pair = weights_now
    tokens = x.shape[0]
    gains_now = model_gains.astype(jnp.float32)
    head_now = head_pair.astype(jnp.float32)
    normed, pull_in = jax.vjp(rms_scale, x, gains_now[0])
    hidden = normed.astype(jnp.bfloat16)
    raw_all = jnp.dot(hidden, qkv_mat, preferred_element_type=jnp.float32)
    query_raw = raw_all[:, : HEADS * HD]
    key_raw = raw_all[:, HEADS * HD : HEADS * HD + HD]
    values = raw_all[:, HEADS * HD + HD :].astype(jnp.bfloat16)

    def query_piece(raw_vals, gain_vec):
        return rotate(
            rms_scale(raw_vals.reshape(tokens, HEADS, HD), gain_vec),
            cosine[:, None, :],
            sine_part[:, None, :],
        )

    def key_piece(raw_vals, gain_vec):
        return rotate(rms_scale(raw_vals, gain_vec), cosine, sine_part)

    query_rot, pull_query = jax.vjp(query_piece, query_raw, head_now[0])
    key_rot, pull_key = jax.vjp(key_piece, key_raw, head_now[1])
    query_low = query_rot.astype(jnp.bfloat16)
    key_low = key_rot.astype(jnp.bfloat16)
    key_parts = []
    value_parts = []
    for shift_by, rim_rows in rim_sizes(tokens):
        got_both = passed_along(jnp.concatenate([key_low, values], 1), "seq", shift_by)
        key_parts.append(got_both[:, :HD])
        value_parts.append(got_both[:, HD:])
    key_ext = jnp.concatenate(key_parts + [key_low], 0)
    value_ext = jnp.concatenate(value_parts + [values], 0)
    scores, allowed = block_scores(query_low, key_ext, seg_own, seg_ext)
    masked = jnp.where(allowed, scores, -1e30)
    row_top = jnp.max(masked, -1, keepdims=True)
    raised = jnp.where(allowed, jnp.exp(masked - row_top), 0.0)
    row_total = jnp.sum(raised, -1, keepdims=True)
    attention = (raised / row_total).astype(jnp.bfloat16)
    outputs = jnp.einsum("hqk,kd->qhd", attention, value_ext, preferred_element_type=jnp.float32)
    row_tops = [row_top]
    totals = [row_total]
    attended = outputs.reshape(tokens, HEADS * HD).astype(jnp.bfloat16)
    projected = jnp.dot(attended, out_mat, preferred_element_type=jnp.float32)
    post_out, pull_post = jax.vjp(rms_scale, projected, gains_now[1])
    middle = x + post_out
    normed_two, pull_pre = jax.vjp(rms_scale, middle, gains_now[2])
    hidden_two = normed_two.astype(jnp.bfloat16)
    both_vals = jnp.dot(hidden_two, both_mat, preferred_element_type=jnp.float32)
    gate_vals = both_vals[:, : both_vals.shape[1] // 2]
    up_part = both_vals[:, both_vals.shape[1] // 2 :]
    activated, pull_act = jax.vjp(gelu_gate, gate_vals, up_part)
    act_low = activated.astype(jnp.bfloat16)
    ffn_out = jnp.dot(act_low, down_mat, preferred_element_type=jnp.float32)
    post_two, pull_ffn = jax.vjp(rms_scale, ffn_out, gains_now[3])
    retained = (
        hidden,
        query_low,
        key_ext,
        value_ext,
        row_tops,
        totals,
        attended,
        hidden_two,
        act_low,
        pull_in,
        pull_query,
        pull_key,
        pull_post,
        pull_pre,
        pull_act,
        pull_ffn,
    )
    return (middle + post_two, retained)


def backward_layer(upstream, weights_now, retained, seg_own, seg_ext):
    qkv_mat, out_mat, both_mat, down_mat, model_gains, head_pair = weights_now
    (
        hidden,
        query_low,
        key_ext,
        value_ext,
        row_tops,
        totals,
        attended,
        hidden_two,
        act_low,
        pull_in,
        pull_query,
        pull_key,
        pull_post,
        pull_pre,
        pull_act,
        pull_ffn,
    ) = retained
    tokens = upstream.shape[0]
    block_rows = min(512, tokens)
    grad_ffn, gain_ffn = pull_ffn(upstream)
    ffn_low = grad_ffn.astype(jnp.bfloat16)
    down_term = outer_sum(act_low, ffn_low).astype(jnp.bfloat16)
    grad_act = back_dot(ffn_low, down_mat)
    grad_gate, grad_up = pull_act(grad_act)
    gate_low = grad_gate.astype(jnp.bfloat16)
    up_low = grad_up.astype(jnp.bfloat16)
    both_low = jnp.concatenate([gate_low, up_low], 1)
    gate_term = outer_sum(hidden_two, gate_low).astype(jnp.bfloat16)
    up_term = outer_sum(hidden_two, up_low).astype(jnp.bfloat16)
    grad_hidden_two = back_dot(both_low, both_mat)
    middle_part, gain_pre = pull_pre(grad_hidden_two)
    grad_middle = upstream + middle_part
    grad_proj, gain_post = pull_post(grad_middle)
    proj_low = grad_proj.astype(jnp.bfloat16)
    out_term = outer_sum(attended, proj_low).astype(jnp.bfloat16)
    grad_att = back_dot(proj_low, out_mat).astype(jnp.bfloat16).reshape(tokens, HEADS, HD)
    key_back = jnp.zeros(key_ext.shape, jnp.float32)
    value_back = jnp.zeros(value_ext.shape, jnp.float32)
    query_parts = []
    for number, begin_at in enumerate(range(0, tokens, block_rows)):
        span_keys = block_rows + WINDOW
        scores, allowed = block_scores(query_low, key_ext, seg_own, seg_ext)
        masked = jnp.where(allowed, scores, -1e30)
        raised = jnp.where(allowed, jnp.exp(masked - row_tops[number]), 0.0)
        attention = raised / totals[number]
        attention_low = attention.astype(jnp.bfloat16)
        grad_prob = jnp.einsum(
            "qhd,kd->hqk", grad_att, value_ext, preferred_element_type=jnp.float32
        )
        spread = jnp.sum(grad_prob * attention, -1, keepdims=True)
        grad_scores = (attention * (grad_prob - spread)).astype(jnp.bfloat16)
        query_parts.append(
            jnp.einsum("hqk,kd->qhd", grad_scores, key_ext, preferred_element_type=jnp.float32)
            * HD ** (-0.5)
        )
        key_back = key_back.at[begin_at : begin_at + span_keys].add(
            jnp.einsum("hqk,qhd->kd", grad_scores, query_low, preferred_element_type=jnp.float32)
            * HD ** (-0.5)
        )
        value_back = value_back.at[begin_at : begin_at + span_keys].add(
            jnp.einsum("hqk,qhd->kd", attention_low, grad_att, preferred_element_type=jnp.float32)
        )
    key_own = key_back[WINDOW:]
    value_own = value_back[WINDOW:]
    offset = 0
    for shift_by, rim_rows in rim_sizes(tokens):
        backs = (key_back[offset : offset + rim_rows], value_back[offset : offset + rim_rows])
        got_both = passed_along(
            jnp.concatenate(backs, 1).astype(jnp.bfloat16), "seq", -shift_by
        ).astype(jnp.float32)
        got_key, got_value = got_both[:, :HD], got_both[:, HD:]
        key_own = key_own.at[tokens - rim_rows :].add(got_key)
        value_own = value_own.at[tokens - rim_rows :].add(got_value)
        offset = offset + rim_rows
    grad_query, gain_query = pull_query(query_parts[0])
    grad_key, gain_key = pull_key(key_own)
    qkv_low = jnp.concatenate(
        [
            grad_query.astype(jnp.bfloat16),
            grad_key.astype(jnp.bfloat16),
            value_own.astype(jnp.bfloat16),
        ],
        1,
    )
    qkv_term = outer_sum(hidden, qkv_low).astype(jnp.bfloat16)
    grad_hidden = back_dot(qkv_low, qkv_mat)
    grad_input, gain_in = pull_in(grad_hidden)
    fsdp_size = lax.axis_size("fsdp")
    width = qkv_term.shape[0] // fsdp_size
    head_terms = jnp.stack([gain_query, gain_key]).T.reshape(fsdp_size, -1, 2)
    head_terms = jnp.pad(head_terms, ((0, 0), (0, width - head_terms.shape[1]), (0, 0)))
    gain_terms = jnp.concatenate(
        [
            jnp.stack([gain_in, gain_post, gain_pre, gain_ffn]).T,
            head_terms.reshape(fsdp_size * width, 2),
        ],
        1,
    ).astype(jnp.bfloat16)
    used = qkv_term.shape[1] + 6
    padding = -used % 1024
    qkv_term = jnp.concatenate(
        [qkv_term, gain_terms, jnp.zeros((fsdp_size * width, padding), jnp.bfloat16)], 1
    )
    return (grad_middle + grad_input, [gate_term, up_term, down_term, qkv_term, out_term])


def split_sums(sums, head_width):
    gate_grad, up_grad, down_grad, qkv_grad, out_grad = sums
    query_cols = HEADS * HD
    gain_at = query_cols + 2 * HD
    shards = (
        qkv_grad[:, :query_cols],
        qkv_grad[:, query_cols : query_cols + HD],
        qkv_grad[:, query_cols + HD : gain_at],
        out_grad,
        gate_grad,
        up_grad,
        down_grad,
    )
    model_shard = qkv_grad[:, gain_at : gain_at + 4].T
    head_shard = qkv_grad[:head_width, gain_at + 4 : gain_at + 6].T
    return (shards, model_shard, head_shard)


def local(
    activations,
    segments,
    positions,
    cotangent,
    query_weight,
    key_weight,
    value_weight,
    out_weight,
    gate_weight,
    up_weight,
    down_weight,
    norm_gains,
    head_gains,
):
    tokens = activations.shape[1]
    layers = query_weight.shape[0]
    fsdp_size = lax.axis_size("fsdp")
    seg_own = segments[0]
    seg_parts = []
    for shift_by, rim_rows in rim_sizes(tokens):
        seg_parts.append(passed_along(seg_own + 1, "seq", shift_by) - 1)
    seg_ext = jnp.concatenate(seg_parts + [seg_own], 0)
    cosine, sine_part = angles(positions[0])
    stream = activations[0].astype(jnp.float32)
    width = norm_gains.shape[2]
    head_width = head_gains.shape[2]
    gain_cols = jnp.concatenate(
        [
            norm_gains.reshape(layers * 4, width).T,
            jnp.pad(head_gains.reshape(layers * 2, head_width).T, ((0, width - head_width), (0, 0))),
        ],
        1,
    )

    def gathered(part):
        return lax.all_gather(part, "fsdp", axis=0, tiled=True)

    stored = []
    for layer_at in range(layers):
        qkv_parts = [query_weight[layer_at], key_weight[layer_at], value_weight[layer_at]]
        if layer_at == 0:
            qkv_parts.append(gain_cols)
        qkv_mat = gathered(jnp.concatenate(qkv_parts, 1))
        if layer_at == 0:
            gains_all = qkv_mat[:, (HEADS + 2) * HD :].astype(jnp.float32)
            model_all = gains_all[:, : layers * 4].T.reshape(layers, 4, -1)
            head_all = gains_all.reshape(fsdp_size, width, -1)[:, :head_width, layers * 4 :]
            head_all = head_all.reshape(HD, layers * 2).T.reshape(layers, 2, HD)
            qkv_mat = qkv_mat[:, : (HEADS + 2) * HD]
        weights_now = (
            qkv_mat,
            gathered(out_weight[layer_at]),
            gathered(jnp.concatenate([gate_weight[layer_at], up_weight[layer_at]], 1)),
            gathered(down_weight[layer_at]),
            model_all[layer_at],
            head_all[layer_at],
        )
        stream, retained = forward_layer(stream, weights_now, seg_own, seg_ext, cosine, sine_part)
        stored.append((weights_now, retained))
    output = stream.astype(jnp.bfloat16)
    upstream = cotangent[0].astype(jnp.float32)
    collected = [None] * layers
    all_terms = []
    for layer_at in range(layers - 1, -1, -1):
        weights_now, retained = stored[layer_at]
        upstream, terms = backward_layer(upstream, weights_now, retained, seg_own, seg_ext)
        all_terms.extend(terms)
    sums = summed_shards(all_terms)
    for layer_at in range(layers):
        from_at = (layers - 1 - layer_at) * len(terms)
        collected[layer_at] = split_sums(sums[from_at : from_at + len(terms)], head_width)
    input_grad = upstream.astype(jnp.bfloat16)
    stacked = [
        jnp.stack([collected[layer_at][0][number] for layer_at in range(layers)])
        for number in range(7)
    ]
    model_grad = jnp.stack([collected[layer_at][1] for layer_at in range(layers)])
    head_grad = jnp.stack([collected[layer_at][2] for layer_at in range(layers)])
    return (
        output[None],
        input_grad[None],
        stacked[0],
        stacked[1],
        stacked[2],
        stacked[3],
        stacked[4],
        stacked[5],
        stacked[6],
        model_grad,
        head_grad,
    )


def solution(mesh):
    placed = (
        P("fsdp", "seq", None),
        P("fsdp", "seq"),
        P("fsdp", "seq"),
        P("fsdp", "seq", None),
        P(None, "fsdp", None),
        P(None, "fsdp", None),
        P(None, "fsdp", None),
        P(None, "fsdp", None),
        P(None, "fsdp", None),
        P(None, "fsdp", None),
        P(None, "fsdp", None),
        P(None, None, "fsdp"),
        P(None, None, "fsdp"),
    )
    return jax.shard_map(
        local,
        mesh=mesh,
        in_specs=placed,
        out_specs=(
            P("fsdp", "seq", None),
            P("fsdp", "seq", None),
            P(None, "fsdp", None),
            P(None, "fsdp", None),
            P(None, "fsdp", None),
            P(None, "fsdp", None),
            P(None, "fsdp", None),
            P(None, "fsdp", None),
            P(None, "fsdp", None),
            P(None, None, "fsdp"),
            P(None, None, "fsdp"),
        ),
        check_vma=False,
    )
```
